1024 devices in a mesh: section: 16 (over z_hi, y), expert: 64 (over z_lo, x, core).
Axes of the slice: x: 4, y: 8, z: 16 (z_hi: 2, z_lo: 8; z = z_hi * 8 + z_lo), core: 2. Of those that a mesh axis runs over, the one named last changes fastest.
Arguments:
- route_ids: int32 [1, 16, 4096, 1], P(None, 'section', 'expert'), may hold values from 0 to 15; in each aligned block of 64 rows (0 to 63, 64 to 127, ..., all dimensions but the last counted through in order) at most 8 rows name the same one
- route_probs: float32 [1, 16, 4096, 1], P(None, 'section', 'expert'), may hold values from 0.2 to 1
- checkpoints: bfloat16 [1, 16, 4096, 2048], P(None, 'section', 'expert'), may hold values from -6 to 6
- grad_in: bfloat16 [16, 4096, 2048], P('section', 'expert'), may hold values from -6 to 6
- gate_weight: bfloat16 [16, 2048, 12288], P('section', None, 'expert'), may hold values from -0.125 to 0.125
- up_weight: bfloat16 [16, 2048, 12288], P('section', None, 'expert'), may hold values from -0.125 to 0.125
- down_weight: bfloat16 [16, 12288, 2048], P('section', 'expert'), may hold values from -0.21875 to 0.21875
Outputs:
- grad_out: bfloat16 [16, 4096, 2048], P('section', 'expert')
The draws below stay inside these ranges and needn't reach their ends.
Inputs may be any that keep to these rules, and one draw needn't show every extreme that they name: `route_ids`: each token names 1 different experts. In each aligned block of 64 tokens of one step and section (the tokens of one device) no expert is named by more than 8 tokens, and in some block one expert is named by exactly 8.
All inputs are finite; a program needn't handle non-finite values.
Results may differ from the reference program's by a relative error of at most 0.0042.
Values may be sent and summed in bfloat16 or wider, within the bound.
A program may use at most 32 MiB of HBM per device.

```python
import math
import jax
import jax.numpy as jnp
import numpy as np
from jax import lax

D = 2048
FF = 768
SPLIT = 4
TOPW = 1
TOK_DEV = 64
TICKS = 1
FF_DEV = 192
EXP_FL = 16
CAP = 8
SECTIONS = 16
TOKENS = 4096
N_EXPERT = 64


def shard_levels(key, shape, shards, smallest, high):
    level, own = 1.0, jax.random.fold_in(key, 6)
    for position, blocks in shards:
        heights = jnp.exp(jax.random.uniform(jax.random.fold_in(own, position), (blocks,), jnp.float32, smallest / len(shards), high / len(shards)))
        level = level * jnp.repeat(heights, shape[position] // blocks).reshape([-1 if axis == position else 1 for axis in range(len(shape))])
    return level


def assign_block(stream_key, own, number, rows, amount, top, bound, skew):
    ranking = jax.random.permutation(stream_key, amount)
    heavy_load, ordinary = portions_of(amount, rows * top, bound, skew, True), portions_of(amount, rows * top, bound, skew, False)
    places = jnp.arange(amount)

    def named(tallies, offset_by):
        used = int((tallies > 0).sum())
        fixed = max(1, used // 4)
        passed = fixed + (places - fixed + offset_by * (used - fixed)) % max(1, amount - fixed)
        return jnp.zeros((amount,), jnp.int32).at[ranking[jnp.where(places < fixed, places, passed)]].set(jnp.asarray(tallies, jnp.int32))

    tallies = jnp.where(number % 4 == 0, named(heavy_load, number // 4), named(ordinary, number - number // 4 - 1))
    mixed = jax.random.permutation(jax.random.fold_in(own, 3), amount)
    donor, receiver = mixed[0:amount // 2 * 2:2], mixed[1:amount // 2 * 2:2]
    slack = jnp.minimum(tallies[donor] - 1, bound - tallies[receiver]) // 2
    slack = jnp.where((donor == ranking[0]) | (receiver == ranking[0]) | (tallies[receiver] == 0), 0, jnp.maximum(slack, 0))
    passed = jax.random.randint(jax.random.fold_in(own, 4), (amount // 2,), 0, 1 << 20) % (slack + 1)
    tallies = tallies.at[donor].add(-passed).at[receiver].add(passed)
    items = jnp.searchsorted(jnp.cumsum(tallies), jnp.arange(rows * top), side="right").astype(jnp.int32)
    table = items.reshape(top, rows).T
    table = table[jax.random.permutation(jax.random.fold_in(own, 1), rows)]
    offset_by = jax.random.randint(jax.random.fold_in(own, 2), (rows, 1), 0, top)
    return jnp.take_along_axis(table, (jnp.arange(top)[None, :] + offset_by) % top, axis=1)


def portions_of(number_of, total, most, lean, full):
    weights = [(1 << 20) // math.isqrt(rank ** lean) + 1 for rank in range(1, number_of + 1)]
    largest = most if full else min(most, max(-(-total // number_of), total * weights[0] // sum(weights)))
    least = 1 if total - largest >= number_of - 1 else 0
    holding, surplus = [largest] + [least] * (number_of - 1), total - largest - least * (number_of - 1)
    while surplus > 0:
        free = [i for i in range(1, number_of) if holding[i] < largest] or [i for i in range(1, number_of) if holding[i] < most]
        whole, remaining = sum([weights[i] for i in free]), surplus
        for i in free:
            extra = min(most - holding[i], max(1, remaining * weights[i] // whole), surplus)
            holding[i] = holding[i] + extra
            surplus = surplus - extra
    return np.array(holding)


def centred(rng, extent, width, limit, split=(), kind=jnp.bfloat16):
    level = shard_levels(rng, extent, split, -0.22, 0.18) if split else 1.0
    values = jax.random.normal(rng, extent, jnp.float32) * width * level
    return jnp.minimum(jnp.maximum(values, -limit), limit).astype(kind)


def setup_inputs(seed: int = 0) -> dict:
    streams_of = jax.random.split(jax.random.key(seed), 8)
    route_ids_keys = jax.random.split(jax.random.fold_in(streams_of[0], 1), TICKS * SECTIONS * TOKENS // TOK_DEV)
    route_ids_turns = jax.random.permutation(jax.random.fold_in(streams_of[0], 3), TICKS * SECTIONS * TOKENS // TOK_DEV)
    route_ids = jax.vmap(lambda own, number: assign_block(jax.random.fold_in(streams_of[0], 2), own, number, TOK_DEV, EXP_FL, TOPW, CAP, 2))(route_ids_keys, route_ids_turns).reshape((TICKS, SECTIONS, TOKENS, TOPW))
    route_probs = jnp.clip(0.2 + 0.8 * jax.random.uniform(streams_of[1], (TICKS, SECTIONS, TOKENS, TOPW), jnp.float32) ** shard_levels(streams_of[1], (TICKS, SECTIONS, TOKENS, TOPW), ((1, 16), (2, 64)), -0.2, 0.2), 0.2, 1.0)
    checkpoints = centred(streams_of[2], (TICKS, SECTIONS, TOKENS, D), 1.0, 6.0, ((1, 16), (2, 64)))
    grad_in = centred(streams_of[3], (SECTIONS, TOKENS, D), 1.0, 6.0, ((0, 16), (1, 64)))
    gate_weight = centred(streams_of[4], (SECTIONS, D, EXP_FL * FF), D ** -0.5, 0.125, ((0, 16), (2, 64)))
    up_weight = centred(streams_of[5], (SECTIONS, D, EXP_FL * FF), D ** -0.5, 0.125, ((0, 16), (2, 64)))
    down_weight = centred(streams_of[6], (SECTIONS, EXP_FL * FF, D), FF ** -0.5, 0.21875, ((0, 16), (1, 64)))
    return dict(route_ids=route_ids, route_probs=route_probs, checkpoints=checkpoints, grad_in=grad_in, gate_weight=gate_weight, up_weight=up_weight, down_weight=down_weight)


def block_slots(block_ids):
    pair_ids = block_ids.reshape(-1)
    onehot = (pair_ids[:, None] == jnp.arange(EXP_FL, dtype=jnp.int32)[None, :]).astype(jnp.int32)
    earlier = jnp.cumsum(onehot, axis=0) - onehot
    return jnp.sum(earlier * onehot, axis=1).astype(jnp.int32).reshape(block_ids.shape)


def expert_backward(items):
    rows_in, rows_grad, gate_cols, up_cols, down_rows = items
    row_count = rows_in.shape[0]
    pre_gate = jnp.dot(rows_in, gate_cols, preferred_element_type=jnp.float32)
    pre_up = jnp.dot(rows_in, up_cols, preferred_element_type=jnp.float32)
    hidden_grad = jnp.dot(rows_grad, down_rows.T, preferred_element_type=jnp.float32)
    sigmoid_gate = jax.nn.sigmoid(pre_gate)
    gate_coef = (hidden_grad * pre_up * sigmoid_gate * (1.0 + pre_gate * (1.0 - sigmoid_gate))).astype(jnp.bfloat16)
    up_coef = (hidden_grad * pre_gate * sigmoid_gate).astype(jnp.bfloat16)
    gate_split = gate_coef.reshape(row_count, SPLIT, FF_DEV).astype(jnp.float32)
    up_split = up_coef.reshape(row_count, SPLIT, FF_DEV).astype(jnp.float32)
    gate_table = gate_cols.reshape(D, SPLIT, FF_DEV).astype(jnp.float32)
    up_table = up_cols.reshape(D, SPLIT, FF_DEV).astype(jnp.float32)
    shares = jnp.einsum("rsf,dsf->srd", gate_split, gate_table) + jnp.einsum("rsf,dsf->srd", up_split, up_table)
    rounded = lax.optimization_barrier(shares.astype(jnp.bfloat16))
    return jnp.sum(rounded.astype(jnp.float32), axis=0)


def section_update(items):
    ids_section, probs_section, rows_section, grad_section, gate_section, up_section, down_section = items
    ids_blocks = ids_section.reshape(N_EXPERT, TOK_DEV, TOPW)
    slots = jax.vmap(block_slots)(ids_blocks)
    source = jnp.arange(N_EXPERT, dtype=jnp.int32)[:, None, None]
    target = (ids_blocks * (N_EXPERT * CAP) + source * CAP + slots).astype(jnp.int32).reshape(-1)
    total_slots = EXP_FL * N_EXPERT * CAP
    rows_rep = jnp.broadcast_to(rows_section.reshape(N_EXPERT, TOK_DEV, 1, D), (N_EXPERT, TOK_DEV, TOPW, D)).reshape(-1, D)
    grad_rep = jnp.broadcast_to(grad_section.reshape(N_EXPERT, TOK_DEV, 1, D), (N_EXPERT, TOK_DEV, TOPW, D)).reshape(-1, D)
    rows_buffer = jnp.zeros((total_slots, D), jnp.bfloat16).at[target].set(rows_rep).reshape(EXP_FL, N_EXPERT * CAP, D)
    grad_buffer = jnp.zeros((total_slots, D), jnp.bfloat16).at[target].set(grad_rep).reshape(EXP_FL, N_EXPERT * CAP, D)
    gate_experts = gate_section.reshape(D, EXP_FL, FF).transpose(1, 0, 2)
    up_experts = up_section.reshape(D, EXP_FL, FF).transpose(1, 0, 2)
    down_experts = down_section.reshape(EXP_FL, FF, D)
    results = lax.map(expert_backward, (rows_buffer, grad_buffer, gate_experts, up_experts, down_experts))
    row_grad = results.reshape(total_slots, D)[target].reshape(TOKENS, TOPW, D)
    update = grad_section.astype(jnp.float32) + jnp.sum(probs_section[:, :, None] * row_grad, axis=1)
    return update.astype(jnp.bfloat16)


def reference(route_ids, route_probs, checkpoints, grad_in, gate_weight, up_weight, down_weight):
    grad_now = grad_in
    for moment in range(TICKS):
        updates = lax.map(section_update, (route_ids[moment], route_probs[moment], checkpoints[moment], grad_now, gate_weight, up_weight, down_weight))
        grad_now = jnp.roll(updates, -1, axis=0)
    return grad_now
```

```python
import jax
import jax.numpy as jnp
from jax import lax
from jax.experimental import pallas as pl
from jax.experimental.pallas import tpu as pltpu
from jax.sharding import PartitionSpec as P

CAP = 8
BLOCK = 2 * CAP
NZ, NX, NC = 8, 4, 2
EXPERTS = NZ * NX * NC // 4
SECTIONS = 16
FF_DEV = 192
D = 2048
HALF = D // 2
ORDER = (4, 5, 6, 7, 3, 2, 1, 0)
MESH = pl.DeviceIdType.MESH
F32, BF16 = jnp.float32, jnp.bfloat16


def flipped(z, m):
    out = 0
    for bit in (4, 2, 1):
        b = (z // bit) % 2
        out = out + bit * ((1 - b) if m & bit else b)
    return out


def kernel(
    ids_ref, probs_ref, rows_ref, grad_ref, gate_hbm, up_hbm, down_hbm, out_hbm,
    weights, packed, held, shares, from_core, for_x, from_x, returned, back, result, landed,
    load_sem, own_sem, to_sem, at_sem, core_send, core_recv, x_send, x_recv, cross_send, cross_recv,
    rc_send, rc_recv, rx_send, rx_recv, ret_send, ret_recv, ret_own, shift_send, shift_recv, out_sem,
):
    sec = lax.axis_index("section")
    dev = lax.axis_index("expert")
    z, x, c = dev // (NX * NC), (dev // NC) % NX, dev % NC

    def at(zz, xx, cc):
        return {"section": sec, "expert": zz * (NX * NC) + xx * NC + cc}

    other_core = at(z, x, 1 - c)
    other_chip = at(z, x + 1 - 2 * (x % 2), c)
    column = (x, NX - 1 - x)
    peers = [(h, m, at(flipped(z, m), column[h], c)) for h in range(2) for m in ORDER]
    ahead = {"section": (sec + SECTIONS - 1) % SECTIONS, "expert": dev}
    behind = {"section": (sec + 1) % SECTIONS, "expert": dev}

    loads = [
        pltpu.make_async_copy(src, weights.at[pl.ds(i * FF_DEV, FF_DEV)], load_sem.at[i])
        for i, src in enumerate((gate_hbm, up_hbm, down_hbm))
    ]
    for load in loads:
        load.start()

    barrier = pltpu.get_barrier_semaphore()
    partners = [p for h, m, p in peers if (h, m) != (0, 0)] + [other_core, other_chip, ahead, behind]
    for partner in partners:
        pl.semaphore_signal(barrier, inc=1, device_id=partner, device_id_type=MESH)

    ids = ids_ref[...]
    tokens = ids.shape[1]
    named = (lax.broadcasted_iota(jnp.int32, (EXPERTS, tokens), 0) == ids).astype(F32)
    before = (
        lax.broadcasted_iota(jnp.int32, (tokens, tokens), 0)
        < lax.broadcasted_iota(jnp.int32, (tokens, tokens), 1)
    ).astype(F32)
    earlier = jnp.dot(named, before, preferred_element_type=F32)
    rank = jnp.sum(earlier * named, axis=0, keepdims=True).astype(jnp.int32)
    message = jnp.where(ids % 2 == x // 2, 0, NZ) + jnp.bitwise_xor(ids // 2, z)
    place = message * BLOCK + rank
    row = lax.broadcasted_iota(jnp.int32, (EXPERTS * BLOCK, tokens), 0)
    pick = jnp.concatenate(
        [(row == place).astype(F32), (row == place + CAP).astype(F32)], axis=1
    ).astype(BF16)
    pair = jnp.concatenate([rows_ref[...], grad_ref[...]], axis=0)
    for n in range(0, D, 512):
        packed[:, :, n : n + 512] = (
            jnp.dot(pick, pair[:, n : n + 512], preferred_element_type=F32)
            .astype(BF16)
            .reshape(EXPERTS, BLOCK, 512)
        )

    pl.semaphore_wait(barrier, len(partners))

    sends = []
    for h, m, peer in peers:
        i = h * NZ + m
        if (h, m) == (0, 0):
            copy = pltpu.make_async_copy(packed.at[i], held.at[0, i], own_sem)
        else:
            copy = pltpu.make_async_remote_copy(
                src_ref=packed.at[i], dst_ref=held.at[0, i], send_sem=to_sem.at[i],
                recv_sem=at_sem.at[i], device_id=peer, device_id_type=MESH,
            )
        copy.start()
        sends.append((h, m, i, copy))

    for load in loads:
        load.wait()

    def forward(quarter, to, i, send, recv, device):
        return pltpu.make_async_remote_copy(
            src_ref=held.at[quarter, i], dst_ref=held.at[to, i], send_sem=send.at[i],
            recv_sem=recv.at[i], device_id=device, device_id_type=MESH,
        )

    def rows_of(h, first):
        block = held[:, h * NZ : (h + 1) * NZ, first : first + CAP, :]
        return block.reshape(4 * NZ * CAP, D)

    contract = (((1,), (1,)), ((), ()))
    chunk = NZ * CAP
    returns = []
    for h in range(2):
        mine = [s for s in sends if s[0] == h]
        on_core, on_x, on_cross = [], [], []
        for _, m, i, copy in mine:
            if (h, m) == (0, 0):
                copy.wait()
            else:
                copy.wait_recv()
            over = forward(0, 2, i, x_send, x_recv, other_chip)
            over.start()
            on_x.append(over)
            over = forward(0, 1, i, core_send, core_recv, other_core)
            over.start()
            on_core.append(over)
        for (_, m, i, _), over in zip(mine, on_x):
            over.wait_recv()
            cross = forward(2, 3, i, cross_send, cross_recv, other_core)
            cross.start()
            on_cross.append(cross)
        for over in on_core + on_cross:
            over.wait_recv()

        rows_in = rows_of(h, 0)
        rows_grad = rows_of(h, CAP)
        pre_gate = lax.dot_general(rows_in, weights[0:FF_DEV], contract, preferred_element_type=F32)
        pre_up = lax.dot_general(
            rows_in, weights[FF_DEV : 2 * FF_DEV], contract, preferred_element_type=F32
        )
        hidden = lax.dot_general(
            rows_grad, weights[2 * FF_DEV : 3 * FF_DEV], contract, preferred_element_type=F32
        )
        g = jax.nn.sigmoid(pre_gate)
        gate_coef = (hidden * pre_up * g * (1.0 + pre_gate * (1.0 - g))).astype(BF16)
        up_coef = (hidden * pre_gate * g).astype(BF16)
        for n in range(0, D, 512):
            total = jnp.dot(gate_coef, weights[0:FF_DEV, n : n + 512], preferred_element_type=F32)
            total = total + jnp.dot(
                up_coef, weights[FF_DEV : 2 * FF_DEV, n : n + 512], preferred_element_type=F32
            )
            shares[h, :, :, n : n + 512] = total.astype(BF16).reshape(4, chunk, 512)

        to_core = []
        for j, quarter in enumerate((3, 1)):
            copy = pltpu.make_async_remote_copy(
                src_ref=shares.at[h, quarter], dst_ref=from_core.at[h, j],
                send_sem=rc_send.at[h, j], recv_sem=rc_recv.at[h, j],
                device_id=other_core, device_id_type=MESH,
            )
            copy.start()
            to_core.append(copy)
        to_core[0].wait_recv()
        for_x[h] = (shares[h, 2].astype(F32) + from_core[h, 0].astype(F32)).astype(BF16)
        to_x = pltpu.make_async_remote_copy(
            src_ref=for_x.at[h], dst_ref=from_x.at[h], send_sem=rx_send.at[h],
            recv_sem=rx_recv.at[h], device_id=other_chip, device_id_type=MESH,
        )
        to_x.start()
        to_core[1].wait_recv()
        to_x.wait_recv()
        total = shares[h, 0].astype(F32) + from_core[h, 1].astype(F32) + from_x[h].astype(F32)
        total = total.astype(BF16).reshape(NZ, CAP, D)
        returned[h, :, 0:CAP, :] = total[:, :, 0:HALF]
        returned[h, :, CAP:BLOCK, :] = total[:, :, HALF:D]
        for _, m, peer in peers[h * NZ : (h + 1) * NZ]:
            if (h, m) == (0, 0):
                copy = pltpu.make_async_copy(returned.at[h, m], back.at[h, m], ret_own)
            else:
                copy = pltpu.make_async_remote_copy(
                    src_ref=returned.at[h, m], dst_ref=back.at[h, m],
                    send_sem=ret_send.at[h, m], recv_sem=ret_recv.at[h, m],
                    device_id=peer, device_id_type=MESH,
                )
            copy.start()
            returns.append((h, m, copy))
        for copy in to_core + [to_x] + on_core + on_x + on_cross:
            copy.wait_send()

    for h, m, copy in returns:
        if (h, m) == (0, 0):
            copy.wait()
        else:
            copy.wait_recv()

    eye = lax.broadcasted_iota(jnp.int32, (tokens, tokens), 0) == lax.broadcasted_iota(
        jnp.int32, (tokens, tokens), 1
    )
    place_col = jnp.sum(jnp.where(eye, place, 0), axis=1, keepdims=True)
    prob_col = jnp.sum(jnp.where(eye, probs_ref[...], 0.0), axis=1, keepdims=True)
    slot = lax.broadcasted_iota(jnp.int32, (tokens, EXPERTS * BLOCK), 1)
    rows_back = back[...].reshape(EXPERTS * BLOCK, HALF)
    for side in range(2):
        select = (slot == place_col + side * CAP).astype(BF16)
        own = jnp.dot(select, rows_back, preferred_element_type=F32)
        here = grad_ref[:, side * HALF : (side + 1) * HALF].astype(F32)
        result[side] = (here + prob_col * own).astype(BF16)
        shift = pltpu.make_async_remote_copy(
            src_ref=result.at[side], dst_ref=landed.at[side], send_sem=shift_send.at[side],
            recv_sem=shift_recv.at[side], device_id=ahead, device_id_type=MESH,
        )
        shift.start()
    outs = []
    for side in range(2):
        shift = pltpu.make_async_remote_copy(
            src_ref=result.at[side], dst_ref=landed.at[side], send_sem=shift_send.at[side],
            recv_sem=shift_recv.at[side], device_id=ahead, device_id_type=MESH,
        )
        shift.wait()
        out = pltpu.make_async_copy(
            landed.at[side], out_hbm.at[:, pl.ds(side * HALF, HALF)], out_sem.at[side]
        )
        out.start()
        outs.append(out)
    for h, m, i, copy in sends:
        if (h, m) != (0, 0):
            copy.wait_send()
    for h, m, copy in returns:
        if (h, m) != (0, 0):
            copy.wait_send()
    for out in outs:
        out.wait()


def local(route_ids, route_probs, checkpoints, grad_in, gate_weight, up_weight, down_weight):
    tokens = route_ids.shape[2]
    dma = pltpu.SemaphoreType.DMA
    vmem = pl.BlockSpec(memory_space=pltpu.VMEM)
    hbm = pl.BlockSpec(memory_space=pl.ANY)
    out = pl.pallas_call(
        kernel,
        out_shape=jax.ShapeDtypeStruct((tokens, D), BF16),
        in_specs=[vmem] * 4 + [hbm] * 3,
        out_specs=hbm,
        scratch_shapes=[
            pltpu.VMEM((3 * FF_DEV, D), BF16),
            pltpu.VMEM((EXPERTS, BLOCK, D), BF16),
            pltpu.VMEM((4, EXPERTS, BLOCK, D), BF16),
            pltpu.VMEM((2, 4, NZ * CAP, D), BF16),
            pltpu.VMEM((2, 2, NZ * CAP, D), BF16),
            pltpu.VMEM((2, NZ * CAP, D), BF16),
            pltpu.VMEM((2, NZ * CAP, D), BF16),
            pltpu.VMEM((2, NZ, BLOCK, HALF), BF16),
            pltpu.VMEM((2, NZ, BLOCK, HALF), BF16),
            pltpu.VMEM((2, tokens, HALF), BF16),
            pltpu.VMEM((2, tokens, HALF), BF16),
            dma((3,)), dma, dma((16,)), dma((16,)),
            dma((16,)), dma((16,)), dma((16,)), dma((16,)), dma((16,)), dma((16,)),
            dma((2, 2)), dma((2, 2)), dma((2,)), dma((2,)),
            dma((2, NZ)), dma((2, NZ)), dma, dma((2,)), dma((2,)), dma((2,)),
        ],
        compiler_params=pltpu.CompilerParams(
            collective_id=0, has_side_effects=True, vmem_limit_bytes=48 * 1024 * 1024
        ),
        cost_estimate=pl.CostEstimate(
            flops=2 * 512 * D * FF_DEV * 5, bytes_accessed=3 * 1024 * 1024, transcendentals=512 * FF_DEV
        ),
    )(
        route_ids.reshape(1, tokens),
        route_probs.reshape(1, tokens),
        checkpoints[0, 0],
        grad_in[0],
        jnp.swapaxes(gate_weight[0], 0, 1),
        jnp.swapaxes(up_weight[0], 0, 1),
        down_weight[0],
    )
    return out[None]


def solution(mesh):
    placed = (
        P(None, "section", "expert", None),
        P(None, "section", "expert", None),
        P(None, "section", "expert", None),
        P("section", "expert", None),
        P("section", None, "expert"),
        P("section", None, "expert"),
        P("section", "expert", None),
    )
    return jax.shard_map(
        local, mesh=mesh, in_specs=placed, out_specs=P("section", "expert", None), check_vma=False
    )
```

```python
import jax
import jax.numpy as jnp
from jax import lax
from jax.experimental import pallas as pl
from jax.experimental.pallas import tpu as pltpu
from jax.sharding import PartitionSpec as P

CAP = 8
BLOCK = 2 * CAP
NZ, NX, NC = 8, 4, 2
EXPERTS = NZ * NX * NC // 4
SECTIONS = 16
FF_DEV = 192
D = 2048
HALF = D // 2
QUAD = D // 4
NY = 8
PIECE = 16
CHUNKS = ((0, 4), (0, 0), (1, 0), (1, 4))
ORDER = (
    (0, 4), (0, 5), (0, 6), (0, 7), (1, 4), (0, 3), (0, 2), (1, 5),
    (0, 1), (0, 0), (1, 6), (1, 3), (1, 2), (1, 7), (1, 1), (1, 0),
)
WIDE = 4
CROWS = WIDE * CAP
MESH = pl.DeviceIdType.MESH
F32, BF16 = jnp.float32, jnp.bfloat16


def flipped(z, m):
    out = 0
    for bit in (4, 2, 1):
        b = (z // bit) % 2
        out = out + bit * ((1 - b) if m & bit else b)
    return out


def kernel(
    ids_ref, probs_ref, rows_hbm, grad_hbm, gate_hbm, up_hbm, down_hbm, out_hbm,
    weights, pair, packed, held, shares, from_core, for_x, from_x, returned, back, result, relay,
    load_sem, pair_sem, own_sem, to_sem, at_sem, x_send, x_recv, core_send, core_recv,
    rc_send, rc_recv, rx_send, rx_recv, ret_send, ret_recv, ret_own,
    shift_send, shift_recv, leg_send, leg_recv, end_send, end_recv,
):
    sec = lax.axis_index("section")
    dev = lax.axis_index("expert")
    z, x, c = dev // (NX * NC), (dev // NC) % NX, dev % NC
    y = sec % NY
    depth = (sec // NY) * NZ + z
    tokens = ids_ref.shape[1]

    def at(zz, xx, cc):
        return {"section": sec, "expert": zz * (NX * NC) + xx * NC + cc}

    def ring(yy, by):
        d = (depth + by + 2 * NZ) % (2 * NZ)
        return {
            "section": (d // NZ) * NY + yy,
            "expert": (d % NZ) * (NX * NC) + x * NC + c,
        }

    def remote(src, dst, send, recv, device):
        return pltpu.make_async_remote_copy(
            src_ref=src, dst_ref=dst, send_sem=send, recv_sem=recv,
            device_id=device, device_id_type=MESH,
        )

    other_core = at(z, x, 1 - c)
    other_chip = at(z, x + 1 - 2 * (x % 2), c)
    column = (x, NX - 1 - x)
    peers = {(h, m): at(flipped(z, m), column[h], c) for h, m in ORDER}
    ahead = {"section": (sec + SECTIONS - 1) % SECTIONS, "expert": dev}
    behind = {"section": (sec + 1) % SECTIONS, "expert": dev}
    first, last = y == 0, y == NY - 1
    edge = first | last

    barrier = pltpu.get_barrier_semaphore()

    def greet(device):
        pl.semaphore_signal(barrier, inc=1, device_id=device, device_id_type=MESH)

    partners = [peers[k] for k in ORDER if k != (0, 0)] + [other_core, other_chip]
    for partner in partners:
        greet(partner)

    @pl.when(y > 0)
    def _():
        greet(ahead)

    @pl.when(y < NY - 1)
    def _():
        greet(behind)

    @pl.when(edge)
    def _():
        for by in (1, -1):
            greet(ring(y, 7 * by))
            greet(ring(NY - 1 - y, by))

    takes = [
        pltpu.make_async_copy(src, pair.at[pl.ds(i * tokens, tokens)], pair_sem.at[i])
        for i, src in enumerate((rows_hbm, grad_hbm))
    ]
    loads = [
        pltpu.make_async_copy(src, weights.at[pl.ds(i * FF_DEV, FF_DEV)], load_sem.at[i])
        for i, src in enumerate((gate_hbm, up_hbm, down_hbm))
    ]
    for load in takes + loads:
        load.start()

    ids = ids_ref[...]
    named = (lax.broadcasted_iota(jnp.int32, (EXPERTS, tokens), 0) == ids).astype(F32)
    before = (
        lax.broadcasted_iota(jnp.int32, (tokens, tokens), 0)
        < lax.broadcasted_iota(jnp.int32, (tokens, tokens), 1)
    ).astype(F32)
    earlier = jnp.dot(named, before, preferred_element_type=F32)
    rank = jnp.sum(earlier * named, axis=0, keepdims=True).astype(jnp.int32)
    message = jnp.where(ids % 2 == x // 2, 0, NZ) + jnp.bitwise_xor(ids // 2, z)
    place = message * BLOCK + rank
    row = lax.broadcasted_iota(jnp.int32, (EXPERTS * BLOCK, tokens), 0)
    pick = jnp.concatenate(
        [(row == place).astype(F32), (row == place + CAP).astype(F32)], axis=1
    ).astype(BF16)
    for take in takes:
        take.wait()
    for n in range(0, D, QUAD):
        packed[:, :, n : n + QUAD] = (
            jnp.dot(pick, pair[:, n : n + QUAD], preferred_element_type=F32)
            .astype(BF16)
            .reshape(EXPERTS, BLOCK, QUAD)
        )

    @pl.when(edge)
    def _():
        pl.semaphore_wait(barrier, len(partners) + 5)

    @pl.when(jnp.logical_not(edge))
    def _():
        pl.semaphore_wait(barrier, len(partners) + 2)

    sends = {}
    for h, m in ORDER:
        i = h * NZ + m
        if i == 0:
            copy = pltpu.make_async_copy(packed.at[i], held.at[0, i], own_sem)
        else:
            copy = remote(packed.at[i], held.at[0, i], to_sem.at[i], at_sem.at[i], peers[h, m])
        copy.start()
        sends[i] = copy

    for load in loads:
        load.wait()

    contract = (((1,), (1,)), ((), ()))
    unsent = []

    def gather(k):
        h, m0 = CHUNKS[k]
        i0 = h * NZ + m0
        over_x = []
        for i in range(i0 + WIDE - 1, i0 - 1, -1) if m0 == 0 else range(i0, i0 + WIDE):
            if i == 0:
                sends[i].wait()
            else:
                sends[i].wait_recv()
            copy = remote(held.at[0, i], held.at[2, i], x_send.at[i], x_recv.at[i], other_chip)
            copy.start()
            over_x.append(copy)
        many = pl.ds(i0, WIDE)
        own = remote(held.at[0, many], held.at[1, many], core_send.at[k, 0], core_recv.at[k, 0], other_core)
        own.start()
        for copy in over_x:
            copy.wait_recv()
        cross = remote(held.at[2, many], held.at[3, many], core_send.at[k, 1], core_recv.at[k, 1], other_core)
        cross.start()
        own.wait_recv()
        cross.wait_recv()
        unsent.extend(over_x + [own, cross])

    def compute(k):
        h, m0 = CHUNKS[k]
        i0 = h * NZ + m0

        def rows_of(top):
            return held[:, i0 : i0 + WIDE, top : top + CAP, :].reshape(4 * CROWS, D)

        rows_in, rows_grad = rows_of(0), rows_of(CAP)
        pre_gate = lax.dot_general(rows_in, weights[0:FF_DEV], contract, preferred_element_type=F32)
        pre_up = lax.dot_general(
            rows_in, weights[FF_DEV : 2 * FF_DEV], contract, preferred_element_type=F32
        )
        hidden = lax.dot_general(
            rows_grad, weights[2 * FF_DEV : 3 * FF_DEV], contract, preferred_element_type=F32
        )
        g = jax.nn.sigmoid(pre_gate)
        gate_coef = (hidden * pre_up * g * (1.0 + pre_gate * (1.0 - g))).astype(BF16)
        up_coef = (hidden * pre_gate * g).astype(BF16)
        for n in range(0, D, QUAD):
            total = jnp.dot(gate_coef, weights[0:FF_DEV, n : n + QUAD], preferred_element_type=F32)
            total = total + jnp.dot(
                up_coef, weights[FF_DEV : 2 * FF_DEV, n : n + QUAD], preferred_element_type=F32
            )
            shares[k, :, :, n : n + QUAD] = total.astype(BF16).reshape(4, CROWS, QUAD)
        for j, quarter in enumerate((3, 1)):
            copy = to_core(k, j, quarter)
            copy.start()
            unsent.append(copy)

    def to_core(k, j, quarter):
        return remote(
            shares.at[k, quarter], from_core.at[k, j], rc_send.at[k, j], rc_recv.at[k, j], other_core
        )

    def to_chip(k):
        return remote(for_x.at[k], from_x.at[k], rx_send.at[k], rx_recv.at[k], other_chip)

    def reduce(k):
        to_core(k, 0, 3).wait_recv()
        for_x[k] = (shares[k, 2].astype(F32) + from_core[k, 0].astype(F32)).astype(BF16)
        copy = to_chip(k)
        copy.start()
        unsent.append(copy)

    returns = {}

    def give_back(k):
        h, m0 = CHUNKS[k]
        to_core(k, 1, 1).wait_recv()
        to_chip(k).wait_recv()
        for side in range(2):
            for half in range(2):
                n = side * HALF + half * QUAD
                total = (
                    shares[k, 0, :, n : n + QUAD].astype(F32)
                    + from_core[k, 1, :, n : n + QUAD].astype(F32)
                    + from_x[k, :, n : n + QUAD].astype(F32)
                )
                returned[side, k, :, half * CAP : (half + 1) * CAP, :] = total.astype(BF16).reshape(
                    WIDE, CAP, QUAD
                )
            for j in range(WIDE):
                m = m0 + j
                i = h * NZ + m
                src, dst = returned.at[side, k, j], back.at[side, i]
                if i == 0:
                    copy = pltpu.make_async_copy(src, dst, ret_own.at[side])
                else:
                    copy = remote(src, dst, ret_send.at[side, i], ret_recv.at[side, i], peers[h, m])
                copy.start()
                returns[side, i] = copy

    gather(0)
    compute(0)
    reduce(0)
    gather(1)
    give_back(0)
    compute(1)
    reduce(1)
    gather(2)
    give_back(1)
    compute(2)
    reduce(2)
    give_back(2)
    gather(3)
    compute(3)
    reduce(3)
    give_back(3)

    eye = lax.broadcasted_iota(jnp.int32, (tokens, tokens), 0) == lax.broadcasted_iota(
        jnp.int32, (tokens, tokens), 1
    )
    place_col = jnp.sum(jnp.where(eye, place, 0), axis=1, keepdims=True)
    prob_col = jnp.sum(jnp.where(eye, probs_ref[...], 0.0), axis=1, keepdims=True)
    slot = lax.broadcasted_iota(jnp.int32, (tokens, EXPERTS * BLOCK), 1)

    def piece(ref, side, p):
        return ref.at[pl.ds(p * PIECE, PIECE), pl.ds(side * HALF, HALF)]

    def whole(side):
        cols = pl.ds(side * HALF, HALF)
        return remote(
            result.at[:, cols], out_hbm.at[:, cols], shift_send.at[side], shift_recv.at[side], ahead
        )

    def leg(side, j, by, plane):
        p = 2 * plane + j
        way = ring(NY - 1, by) if plane else ring(0, 7 * by)
        return remote(
            piece(result, side, p), relay.at[side, j], leg_send.at[side, p], leg_recv.at[side, j], way
        )

    def end(side, j, by, plane):
        p = 2 * plane + j
        way = ring(NY - 1, 7 * by if plane else by)
        return remote(
            relay.at[side, j], piece(out_hbm, side, p), end_send.at[side, j], end_recv.at[side, p], way
        )

    ways = ((0, 1), (1, -1))

    def combine(side):
        for i in range(EXPERTS):
            if i == 0:
                returns[side, i].wait()
            else:
                returns[side, i].wait_recv()
        rows_back = back[side].reshape(EXPERTS * BLOCK, QUAD)
        for half in range(2):
            n = side * HALF + half * QUAD
            select = (slot == place_col + half * CAP).astype(BF16)
            own = jnp.dot(select, rows_back, preferred_element_type=F32)
            here = pair[tokens : 2 * tokens, n : n + QUAD].astype(F32)
            result[:, n : n + QUAD] = (here + prob_col * own).astype(BF16)

        @pl.when(jnp.logical_not(first))
        def _():
            whole(side).start()

        @pl.when(first)
        def _():
            for j, by in ways:
                for plane in range(2):
                    leg(side, j, by, plane).start()

    def pass_on(side, plane):
        for j, by in ways:
            leg(side, j, by, plane).wait_recv()
            end(side, j, by, plane).start()

    combine(0)

    @pl.when(last)
    def _():
        pass_on(0, 1)

    combine(1)

    @pl.when(first)
    def _():
        pass_on(0, 0)
        pass_on(1, 0)

    @pl.when(last)
    def _():
        pass_on(1, 1)

    @pl.when(jnp.logical_not(last))
    def _():
        for side in range(2):
            whole(side).wait_recv()

    @pl.when(last)
    def _():
        for side in range(2):
            for j, by in ways:
                for plane in range(2):
                    end(side, j, by, plane).wait_recv()

    @pl.when(jnp.logical_not(first))
    def _():
        for side in range(2):
            whole(side).wait_send()

    @pl.when(first)
    def _():
        for side in range(2):
            for j, by in ways:
                for plane in range(2):
                    leg(side, j, by, plane).wait_send()
                end(side, j, by, 0).wait_send()

    @pl.when(last)
    def _():
        for side in range(2):
            for j, by in ways:
                end(side, j, by, 1).wait_send()

    for copy in unsent:
        copy.wait_send()
    for i, copy in sends.items():
        if i:
            copy.wait_send()
    for (side, i), copy in returns.items():
        if i:
            copy.wait_send()


def local(route_ids, route_probs, checkpoints, grad_in, gate_weight, up_weight, down_weight):
    tokens = route_ids.shape[2]
    dma = pltpu.SemaphoreType.DMA
    vmem = pl.BlockSpec(memory_space=pltpu.VMEM)
    hbm = pl.BlockSpec(memory_space=pl.ANY)
    chunks = len(CHUNKS)
    out = pl.pallas_call(
        kernel,
        out_shape=jax.ShapeDtypeStruct((tokens, D), BF16),
        in_specs=[vmem] * 2 + [hbm] * 5,
        out_specs=hbm,
        scratch_shapes=[
            pltpu.VMEM((3 * FF_DEV, D), BF16),
            pltpu.VMEM((2 * tokens, D), BF16),
            pltpu.VMEM((EXPERTS, BLOCK, D), BF16),
            pltpu.VMEM((4, EXPERTS, BLOCK, D), BF16),
            pltpu.VMEM((chunks, 4, CROWS, D), BF16),
            pltpu.VMEM((chunks, 2, CROWS, D), BF16),
            pltpu.VMEM((chunks, CROWS, D), BF16),
            pltpu.VMEM((chunks, CROWS, D), BF16),
            pltpu.VMEM((2, chunks, WIDE, BLOCK, QUAD), BF16),
            pltpu.VMEM((2, EXPERTS, BLOCK, QUAD), BF16),
            pltpu.VMEM((tokens, D), BF16),
            pltpu.VMEM((2, 2, PIECE, HALF), BF16),
            dma((3,)), dma((2,)), dma, dma((16,)), dma((16,)), dma((16,)), dma((16,)),
            dma((chunks, 2)), dma((chunks, 2)), dma((chunks, 2)), dma((chunks, 2)),
            dma((chunks,)), dma((chunks,)), dma((2, 16)), dma((2, 16)), dma((2,)),
            dma((2,)), dma((2,)), dma((2, 4)), dma((2, 2)), dma((2, 2)), dma((2, 4)),
        ],
        compiler_params=pltpu.CompilerParams(
            collective_id=0, has_side_effects=True, vmem_limit_bytes=60 * 1024 * 1024
        ),
        cost_estimate=pl.CostEstimate(
            flops=2 * 512 * D * FF_DEV * 5, bytes_accessed=3 * 1024 * 1024, transcendentals=512 * FF_DEV
        ),
    )(
        route_ids.reshape(1, tokens),
        route_probs.reshape(1, tokens),
        checkpoints[0, 0],
        grad_in[0],
        jnp.swapaxes(gate_weight[0], 0, 1),
        jnp.swapaxes(up_weight[0], 0, 1),
        down_weight[0],
    )
    return out[None]


def solution(mesh):
    placed = (
        P(None, "section", "expert", None),
        P(None, "section", "expert", None),
        P(None, "section", "expert", None),
        P("section", "expert", None),
        P("section", None, "expert"),
        P("section", None, "expert"),
        P("section", "expert", None),
    )
    return jax.shard_map(
        local, mesh=mesh, in_specs=placed, out_specs=P("section", "expert", None), check_vma=False
    )
```

```python
import jax
import jax.numpy as jnp
from jax import lax
from jax.experimental import pallas as pl
from jax.experimental.pallas import tpu as pltpu
from jax.sharding import PartitionSpec as P

CAP = 8
BLOCK = 2 * CAP
NZ, NX, NC = 8, 4, 2
EXPERTS = NZ * NX * NC // 4
SECTIONS = 16
FF_DEV = 192
D = 2048
HALF = D // 2
QUAD = D // 4
NY = 8
PIECE = 16
PLANES = (0, NY - 1, 1, NY - 2)
NEXT = 1
NEAR = (0, 8, 1, 9, 2, 10, 3, 11)
FAR = (4, 5, 6, 7, 12, 13, 14, 15)
WINDOW = 4
CHUNKS = ((0, 4), (8, 4), (4, 2), (6, 2), (12, 2), (14, 2))
MESH = pl.DeviceIdType.MESH
F32, BF16 = jnp.float32, jnp.bfloat16


def flipped(z, m):
    out = 0
    for bit in (4, 2, 1):
        b = (z // bit) % 2
        out = out + bit * ((1 - b) if m & bit else b)
    return out


def kernel(
    ids_ref, probs_ref, rows_hbm, grad_hbm, gate_hbm, up_hbm, down_hbm, out_hbm,
    weights, pair, packed, held, shares, from_core, for_x, from_x, returned, back, result, relay,
    load_sem, pair_sem, own_sem, to_sem, at_sem, x_send, x_recv, core_send, core_recv,
    rc_send, rc_recv, rx_send, rx_recv, ret_send, ret_recv, ret_own,
    shift_send, shift_recv, leg_send, leg_recv, end_send, end_recv,
):
    sec = lax.axis_index("section")
    dev = lax.axis_index("expert")
    z, x, c = dev // (NX * NC), (dev // NC) % NX, dev % NC
    y = sec % NY
    depth = (sec // NY) * NZ + z
    tokens = ids_ref.shape[1]

    def at(zz, xx, cc):
        return {"section": sec, "expert": zz * (NX * NC) + xx * NC + cc}

    def ring(yy, by):
        d = (depth + by + 2 * NZ) % (2 * NZ)
        return {
            "section": (d // NZ) * NY + yy,
            "expert": (d % NZ) * (NX * NC) + x * NC + c,
        }

    def remote(src, dst, send, recv, device):
        return pltpu.make_async_remote_copy(
            src_ref=src, dst_ref=dst, send_sem=send, recv_sem=recv,
            device_id=device, device_id_type=MESH,
        )

    other_core = at(z, x, 1 - c)
    other_chip = at(z, x + 1 - 2 * (x % 2), c)
    column = (x, NX - 1 - x)
    peers = [at(flipped(z, i % NZ), column[i // NZ], c) for i in range(EXPERTS)]
    ahead = {"section": (sec + SECTIONS - 1) % SECTIONS, "expert": dev}
    behind = {"section": (sec + 1) % SECTIONS, "expert": dev}
    first, last = y == 0, y == NY - 1
    edge = first | last
    relays = edge | (y == 1) | (y == NY - 2)

    barrier = pltpu.get_barrier_semaphore()

    def greet(device):
        pl.semaphore_signal(barrier, inc=1, device_id=device, device_id_type=MESH)

    partners = peers[1:] + [other_core, other_chip]
    for partner in partners:
        greet(partner)

    @pl.when(y > 0)
    def _():
        greet(ahead)

    @pl.when(y < NY - 1)
    def _():
        greet(behind)

    @pl.when(first)
    def _():
        for plane in PLANES:
            for by in (1, -1):
                greet(ring(plane, by * NEXT))

    @pl.when(relays)
    def _():
        for by in (1, -1):
            greet(ring(0, by * NEXT))
            greet(ring(NY - 1, by * (NZ - NEXT)))

    @pl.when(last)
    def _():
        for plane in PLANES:
            for by in (1, -1):
                greet(ring(plane, by * (NZ - NEXT)))

    takes = [
        pltpu.make_async_copy(src, pair.at[pl.ds(i * tokens, tokens)], pair_sem.at[i])
        for i, src in enumerate((rows_hbm, grad_hbm))
    ]
    loads = [
        pltpu.make_async_copy(src, weights.at[pl.ds(i * FF_DEV, FF_DEV)], load_sem.at[i])
        for i, src in enumerate((gate_hbm, up_hbm, down_hbm))
    ]
    for load in takes + loads:
        load.start()

    ids = ids_ref[...]
    named = (lax.broadcasted_iota(jnp.int32, (EXPERTS, tokens), 0) == ids).astype(F32)
    before = (
        lax.broadcasted_iota(jnp.int32, (tokens, tokens), 0)
        < lax.broadcasted_iota(jnp.int32, (tokens, tokens), 1)
    ).astype(F32)
    earlier = jnp.dot(named, before, preferred_element_type=F32)
    rank = jnp.sum(earlier * named, axis=0, keepdims=True).astype(jnp.int32)
    message = jnp.where(ids % 2 == x // 2, 0, NZ) + jnp.bitwise_xor(ids // 2, z)
    place = message * BLOCK + rank
    row = lax.broadcasted_iota(jnp.int32, (EXPERTS * BLOCK, tokens), 0)
    pick = jnp.concatenate(
        [(row == place).astype(F32), (row == place + CAP).astype(F32)], axis=1
    ).astype(BF16)
    for take in takes:
        take.wait()
    for n in range(0, D, QUAD):
        packed[:, :, n : n + QUAD] = (
            jnp.dot(pick, pair[:, n : n + QUAD], preferred_element_type=F32)
            .astype(BF16)
            .reshape(EXPERTS, BLOCK, QUAD)
        )

    pairs = 2 * len(PLANES)

    @pl.when(edge)
    def _():
        pl.semaphore_wait(barrier, len(partners) + pairs + 5)

    @pl.when(relays & jnp.logical_not(edge))
    def _():
        pl.semaphore_wait(barrier, len(partners) + 6)

    @pl.when(jnp.logical_not(relays))
    def _():
        pl.semaphore_wait(barrier, len(partners) + 2)

    sends = [pltpu.make_async_copy(packed.at[0], held.at[0, 0], own_sem)] + [
        remote(packed.at[i], held.at[0, i], to_sem.at[i], at_sem.at[i], peers[i])
        for i in range(1, EXPERTS)
    ]
    over_x = [
        remote(held.at[0, i], held.at[2, i], x_send.at[i], x_recv.at[i], other_chip)
        for i in range(EXPERTS)
    ]
    waiting = list(FAR)

    def send_far():
        if waiting:
            sends[waiting.pop(0)].start()

    for _ in range(WINDOW - 1):
        send_far()
    for i in NEAR:
        sends[i].start()

    for load in loads:
        load.wait()

    def arrive(i):
        if i == 0:
            sends[i].wait()
        else:
            sends[i].wait_recv()
        over_x[i].start()

    def to_core(k, j):
        first_slot, slots = CHUNKS[k]
        many = pl.ds(first_slot, slots)
        return remote(
            held.at[2 * j, many], held.at[2 * j + 1, many], core_send.at[k, j], core_recv.at[k, j], other_core
        )

    def gather(k):
        first_slot, slots = CHUNKS[k]
        for i in range(first_slot, first_slot + slots):
            over_x[i].wait_recv()
        to_core(k, 1).start()
        to_core(k, 0).wait_recv()
        to_core(k, 1).wait_recv()

    contract = (((1,), (1,)), ((), ()))

    def rows_of_chunk(k):
        first_slot, slots = CHUNKS[k]
        return pl.ds(first_slot * CAP, slots * CAP)

    def share_to_core(k, j):
        rows = rows_of_chunk(k)
        return remote(
            shares.at[3 - 2 * j, rows], from_core.at[j, rows], rc_send.at[k, j], rc_recv.at[k, j], other_core
        )

    def sum_to_chip(k):
        rows = rows_of_chunk(k)
        return remote(for_x.at[rows], from_x.at[rows], rx_send.at[k], rx_recv.at[k], other_chip)

    def compute(k):
        first_slot, slots = CHUNKS[k]
        rows = rows_of_chunk(k)

        def rows_of(top):
            block = held[:, first_slot : first_slot + slots, top : top + CAP, :]
            return block.reshape(4 * slots * CAP, D)

        rows_in, rows_grad = rows_of(0), rows_of(CAP)
        pre_gate = lax.dot_general(rows_in, weights[0:FF_DEV], contract, preferred_element_type=F32)
        pre_up = lax.dot_general(
            rows_in, weights[FF_DEV : 2 * FF_DEV], contract, preferred_element_type=F32
        )
        hidden = lax.dot_general(
            rows_grad, weights[2 * FF_DEV : 3 * FF_DEV], contract, preferred_element_type=F32
        )
        g = jax.nn.sigmoid(pre_gate)
        gate_coef = (hidden * pre_up * g * (1.0 + pre_gate * (1.0 - g))).astype(BF16)
        up_coef = (hidden * pre_gate * g).astype(BF16)
        for n in range(0, D, QUAD):
            total = jnp.dot(gate_coef, weights[0:FF_DEV, n : n + QUAD], preferred_element_type=F32)
            total = total + jnp.dot(
                up_coef, weights[FF_DEV : 2 * FF_DEV, n : n + QUAD], preferred_element_type=F32
            )
            shares[:, rows, n : n + QUAD] = total.astype(BF16).reshape(4, slots * CAP, QUAD)
        for j in range(2):
            share_to_core(k, j).start()

    def reduce(k):
        rows = rows_of_chunk(k)
        share_to_core(k, 0).wait_recv()
        for_x[rows] = (shares[2, rows].astype(F32) + from_core[0, rows].astype(F32)).astype(BF16)
        sum_to_chip(k).start()

    def finish(k):
        first_slot, slots = CHUNKS[k]
        rows = rows_of_chunk(k)
        share_to_core(k, 1).wait_recv()
        sum_to_chip(k).wait_recv()
        for q in range(4):
            cols = slice(q * QUAD, (q + 1) * QUAD)
            total = (
                shares[0, rows, cols].astype(F32)
                + from_core[1, rows, cols].astype(F32)
                + from_x[rows, cols].astype(F32)
            )
            top = q % 2 * CAP
            returned[q // 2, first_slot : first_slot + slots, top : top + CAP, :] = total.astype(
                BF16
            ).reshape(slots, CAP, QUAD)

    def one_back(side, i):
        src, dst = returned.at[side, i], back.at[side, i]
        if i == 0:
            return pltpu.make_async_copy(src, dst, ret_own.at[side])
        return remote(src, dst, ret_send.at[side, i], ret_recv.at[side, i], peers[i])

    def give_back(side, k):
        first_slot, slots = CHUNKS[k]
        for i in range(first_slot, first_slot + slots):
            one_back(side, i).start()

    for i in NEAR[0::2]:
        arrive(i)
    to_core(0, 0).start()
    send_far()
    for i in NEAR[1::2]:
        arrive(i)
    to_core(1, 0).start()
    gather(0)
    compute(0)
    gather(1)
    compute(1)
    for k in range(2, 6):
        first_slot, slots = CHUNKS[k]
        for i in range(first_slot, first_slot + slots):
            arrive(i)
            if waiting:
                sends[i].wait_send()
                send_far()
        to_core(k, 0).start()
        if k == 2:
            reduce(0)
            reduce(1)
        else:
            reduce(k - 1)
        if k == 5:
            for n in (2, 3):
                give_back(0, n)
        gather(k)
        compute(k)
        if k == 3:
            for n in (0, 1):
                finish(n)
                for side in range(2):
                    give_back(side, n)
            finish(2)
        if k == 4:
            finish(3)
    finish(4)
    give_back(0, 4)
    reduce(5)
    finish(5)
    give_back(0, 5)
    give_back(1, 2)
    for i in (14, 15):
        one_back(0, i).wait_send()
    for k in (3, 4, 5):
        give_back(1, k)

    eye = lax.broadcasted_iota(jnp.int32, (tokens, tokens), 0) == lax.broadcasted_iota(
        jnp.int32, (tokens, tokens), 1
    )
    place_col = jnp.sum(jnp.where(eye, place, 0), axis=1, keepdims=True)
    prob_col = jnp.sum(jnp.where(eye, probs_ref[...], 0.0), axis=1, keepdims=True)
    slot = lax.broadcasted_iota(jnp.int32, (tokens, EXPERTS * BLOCK), 1)

    def piece(ref, side, p):
        return ref.at[pl.ds(p % 4 * PIECE, PIECE), pl.ds(side * HALF + p // 4 * QUAD, QUAD)]

    def whole(side):
        cols = pl.ds(side * HALF, HALF)
        return remote(
            result.at[:, cols], out_hbm.at[:, cols], shift_send.at[side], shift_recv.at[side], ahead
        )

    def leg(side, n, j, by):
        p = 2 * n + j
        return remote(
            piece(result, side, p), relay.at[side, j], leg_send.at[side, p], leg_recv.at[side, j],
            ring(PLANES[n], by * NEXT),
        )

    def end(side, n, j, by):
        p = 2 * n + j
        return remote(
            relay.at[side, j], piece(out_hbm, side, p), end_send.at[side, j], end_recv.at[side, p],
            ring(NY - 1, by * (NZ - NEXT)),
        )

    ways = ((0, 1), (1, -1))

    def combine(side):
        for i in range(EXPERTS):
            if i == 0:
                one_back(side, i).wait()
            else:
                one_back(side, i).wait_recv()
        rows_back = back[side].reshape(EXPERTS * BLOCK, QUAD)
        for half in range(2):
            n = side * HALF + half * QUAD
            select = (slot == place_col + half * CAP).astype(BF16)
            own = jnp.dot(select, rows_back, preferred_element_type=F32)
            here = pair[tokens : 2 * tokens, n : n + QUAD].astype(F32)
            result[:, n : n + QUAD] = (here + prob_col * own).astype(BF16)

        @pl.when(jnp.logical_not(first))
        def _():
            whole(side).start()

        @pl.when(first)
        def _():
            for j, by in ways:
                for n in range(len(PLANES)):
                    leg(side, n, j, by).start()

    def pass_on(side):
        for n, plane in enumerate(PLANES):

            @pl.when(y == plane)
            def _():
                for j, by in ways:
                    leg(side, n, j, by).wait_recv()
                    end(side, n, j, by).start()

    combine(0)
    pass_on(0)
    combine(1)
    pass_on(1)

    @pl.when(jnp.logical_not(last))
    def _():
        for side in range(2):
            whole(side).wait_recv()

    @pl.when(last)
    def _():
        for side in range(2):
            for j, by in ways:
                for n in range(len(PLANES)):
                    end(side, n, j, by).wait_recv()

    @pl.when(jnp.logical_not(first))
    def _():
        for side in range(2):
            whole(side).wait_send()

    @pl.when(first)
    def _():
        for side in range(2):
            for j, by in ways:
                for n in range(len(PLANES)):
                    leg(side, n, j, by).wait_send()

    @pl.when(relays)
    def _():
        for side in range(2):
            for j, by in ways:
                end(side, 0, j, by).wait_send()

    for k, (first_slot, slots) in enumerate(CHUNKS):
        for j in range(2):
            to_core(k, j).wait_send()
            share_to_core(k, j).wait_send()
        sum_to_chip(k).wait_send()
    for i in range(EXPERTS):
        over_x[i].wait_send()
        if i and not (i in FAR and FAR.index(i) < EXPERTS // 2 - WINDOW):
            sends[i].wait_send()
        for side in range(2):
            if i and not (side == 0 and i in (14, 15)):
                one_back(side, i).wait_send()


def local(route_ids, route_probs, checkpoints, grad_in, gate_weight, up_weight, down_weight):
    tokens = route_ids.shape[2]
    dma = pltpu.SemaphoreType.DMA
    vmem = pl.BlockSpec(memory_space=pltpu.VMEM)
    hbm = pl.BlockSpec(memory_space=pl.ANY)
    chunks = len(CHUNKS)
    out = pl.pallas_call(
        kernel,
        out_shape=jax.ShapeDtypeStruct((tokens, D), BF16),
        in_specs=[vmem] * 2 + [hbm] * 5,
        out_specs=hbm,
        scratch_shapes=[
            pltpu.VMEM((3 * FF_DEV, D), BF16),
            pltpu.VMEM((2 * tokens, D), BF16),
            pltpu.VMEM((EXPERTS, BLOCK, D), BF16),
            pltpu.VMEM((4, EXPERTS, BLOCK, D), BF16),
            pltpu.VMEM((4, EXPERTS * CAP, D), BF16),
            pltpu.VMEM((2, EXPERTS * CAP, D), BF16),
            pltpu.VMEM((EXPERTS * CAP, D), BF16),
            pltpu.VMEM((EXPERTS * CAP, D), BF16),
            pltpu.VMEM((2, EXPERTS, BLOCK, QUAD), BF16),
            pltpu.VMEM((2, EXPERTS, BLOCK, QUAD), BF16),
            pltpu.VMEM((tokens, D), BF16),
            pltpu.VMEM((2, 2, PIECE, QUAD), BF16),
            dma((3,)), dma((2,)), dma, dma((16,)), dma((16,)), dma((16,)), dma((16,)),
            dma((chunks, 2)), dma((chunks, 2)), dma((chunks, 2)), dma((chunks, 2)),
            dma((chunks,)), dma((chunks,)), dma((2, 16)), dma((2, 16)), dma((2,)),
            dma((2,)), dma((2,)), dma((2, 8)), dma((2, 2)), dma((2, 2)), dma((2, 8)),
        ],
        compiler_params=pltpu.CompilerParams(
            collective_id=0, has_side_effects=True, vmem_limit_bytes=60 * 1024 * 1024
        ),
        cost_estimate=pl.CostEstimate(
            flops=2 * 512 * D * FF_DEV * 5, bytes_accessed=3 * 1024 * 1024, transcendentals=512 * FF_DEV
        ),
    )(
        route_ids.reshape(1, tokens),
        route_probs.reshape(1, tokens),
        checkpoints[0, 0],
        grad_in[0],
        jnp.swapaxes(gate_weight[0], 0, 1),
        jnp.swapaxes(up_weight[0], 0, 1),
        down_weight[0],
    )
    return out[None]


def solution(mesh):
    placed = (
        P(None, "section", "expert", None),
        P(None, "section", "expert", None),
        P(None, "section", "expert", None),
        P("section", "expert", None),
        P("section", None, "expert"),
        P("section", None, "expert"),
        P("section", "expert", None),
    )
    return jax.shard_map(
        local, mesh=mesh, in_specs=placed, out_specs=P("section", "expert", None), check_vma=False
    )
```

```python
import jax
import jax.numpy as jnp
from jax import lax
from jax.experimental import pallas as pl
from jax.experimental.pallas import tpu as pltpu
from jax.sharding import PartitionSpec as P

CAP = 8
BLOCK = 2 * CAP
NZ, NX, NC = 8, 4, 2
EXPERTS = NZ * NX * NC // 4
SECTIONS = 16
FF_DEV = 192
D = 2048
HALF = D // 2
QUAD = D // 4
NY = 8
PIECE = 16
PLANES = (0, NY - 1, 1, NY - 2)
NEXT = 1
NEAR = (0, 8, 1, 9, 2, 10, 3, 11)
FAR = (4, 5, 6, 7, 12, 13, 14, 15)
WINDOW = 5
CHUNKS = ((0, 4), (8, 4), (4, 2), (6, 2), (12, 2), (14, 2))
MESH = pl.DeviceIdType.MESH
F32, BF16 = jnp.float32, jnp.bfloat16


def flipped(z, m):
    out = 0
    for bit in (4, 2, 1):
        b = (z // bit) % 2
        out = out + bit * ((1 - b) if m & bit else b)
    return out


def kernel(
    ids_ref, probs_ref, rows_hbm, grad_hbm, gate_hbm, up_hbm, down_hbm, out_hbm,
    weights, pair, packed, held, shares, from_core, for_x, from_x, returned, back, result, relay,
    load_sem, pair_sem, own_sem, to_sem, at_sem, x_send, x_recv, core_send, core_recv,
    rc_send, rc_recv, rx_send, rx_recv, ret_send, ret_recv, ret_own,
    shift_send, shift_recv, leg_send, leg_recv, end_send, end_recv,
):
    sec = lax.axis_index("section")
    dev = lax.axis_index("expert")
    z, x, c = dev // (NX * NC), (dev // NC) % NX, dev % NC
    y = sec % NY
    depth = (sec // NY) * NZ + z
    tokens = ids_ref.shape[1]

    def at(zz, xx, cc):
        return {"section": sec, "expert": zz * (NX * NC) + xx * NC + cc}

    def ring(yy, by):
        d = (depth + by + 2 * NZ) % (2 * NZ)
        return {
            "section": (d // NZ) * NY + yy,
            "expert": (d % NZ) * (NX * NC) + x * NC + c,
        }

    def remote(src, dst, send, recv, device):
        return pltpu.make_async_remote_copy(
            src_ref=src, dst_ref=dst, send_sem=send, recv_sem=recv,
            device_id=device, device_id_type=MESH,
        )

    other_core = at(z, x, 1 - c)
    other_chip = at(z, x + 1 - 2 * (x % 2), c)
    column = (x, NX - 1 - x)
    peers = [at(flipped(z, i % NZ), column[i // NZ], c) for i in range(EXPERTS)]
    ahead = {"section": (sec + SECTIONS - 1) % SECTIONS, "expert": dev}
    behind = {"section": (sec + 1) % SECTIONS, "expert": dev}
    first, last = y == 0, y == NY - 1
    edge = first | last
    relays = edge | (y == 1) | (y == NY - 2)

    barrier = pltpu.get_barrier_semaphore()

    def greet(device):
        pl.semaphore_signal(barrier, inc=1, device_id=device, device_id_type=MESH)

    partners = peers[1:] + [other_core, other_chip]
    for partner in partners:
        greet(partner)

    @pl.when(y > 0)
    def _():
        greet(ahead)

    @pl.when(y < NY - 1)
    def _():
        greet(behind)

    @pl.when(first)
    def _():
        for plane in PLANES:
            for by in (1, -1):
                greet(ring(plane, by * NEXT))

    @pl.when(relays)
    def _():
        for by in (1, -1):
            greet(ring(0, by * NEXT))
            greet(ring(NY - 1, by * (NZ - NEXT)))

    @pl.when(last)
    def _():
        for plane in PLANES:
            for by in (1, -1):
                greet(ring(plane, by * (NZ - NEXT)))

    takes = [
        pltpu.make_async_copy(src, pair.at[pl.ds(i * tokens, tokens)], pair_sem.at[i])
        for i, src in enumerate((rows_hbm, grad_hbm))
    ]
    loads = [
        pltpu.make_async_copy(src, weights.at[pl.ds(i * FF_DEV, FF_DEV)], load_sem.at[i])
        for i, src in enumerate((gate_hbm, up_hbm, down_hbm))
    ]
    for load in takes + loads:
        load.start()

    ids = ids_ref[...]
    named = (lax.broadcasted_iota(jnp.int32, (EXPERTS, tokens), 0) == ids).astype(F32)
    before = (
        lax.broadcasted_iota(jnp.int32, (tokens, tokens), 0)
        < lax.broadcasted_iota(jnp.int32, (tokens, tokens), 1)
    ).astype(F32)
    earlier = jnp.dot(named, before, preferred_element_type=F32)
    rank = jnp.sum(earlier * named, axis=0, keepdims=True).astype(jnp.int32)
    message = jnp.where(ids % 2 == x // 2, 0, NZ) + jnp.bitwise_xor(ids // 2, z)
    place = message * BLOCK + rank
    row = lax.broadcasted_iota(jnp.int32, (EXPERTS * BLOCK, tokens), 0)
    pick = jnp.concatenate(
        [(row == place).astype(F32), (row == place + CAP).astype(F32)], axis=1
    ).astype(BF16)
    for take in takes:
        take.wait()
    for n in range(0, D, QUAD):
        packed[:, :, n : n + QUAD] = (
            jnp.dot(pick, pair[:, n : n + QUAD], preferred_element_type=F32)
            .astype(BF16)
            .reshape(EXPERTS, BLOCK, QUAD)
        )

    pairs = 2 * len(PLANES)

    @pl.when(edge)
    def _():
        pl.semaphore_wait(barrier, len(partners) + pairs + 5)

    @pl.when(relays & jnp.logical_not(edge))
    def _():
        pl.semaphore_wait(barrier, len(partners) + 6)

    @pl.when(jnp.logical_not(relays))
    def _():
        pl.semaphore_wait(barrier, len(partners) + 2)

    sends = [pltpu.make_async_copy(packed.at[0], held.at[0, 0], own_sem)] + [
        remote(packed.at[i], held.at[0, i], to_sem.at[i], at_sem.at[i], peers[i])
        for i in range(1, EXPERTS)
    ]
    over_x = [
        remote(held.at[0, i], held.at[2, i], x_send.at[i], x_recv.at[i], other_chip)
        for i in range(EXPERTS)
    ]
    waiting = list(FAR)

    def send_far():
        if waiting:
            sends[waiting.pop(0)].start()

    for _ in range(WINDOW - 1):
        send_far()
    for i in NEAR:
        sends[i].start()

    for load in loads:
        load.wait()

    def arrive(i):
        if i == 0:
            sends[i].wait()
        else:
            sends[i].wait_recv()
        over_x[i].start()

    def to_core(k, j):
        first_slot, slots = CHUNKS[k]
        many = pl.ds(first_slot, slots)
        return remote(
            held.at[2 * j, many], held.at[2 * j + 1, many], core_send.at[k, j], core_recv.at[k, j], other_core
        )

    def gather(k):
        first_slot, slots = CHUNKS[k]
        for i in range(first_slot, first_slot + slots):
            over_x[i].wait_recv()
        to_core(k, 1).start()
        to_core(k, 0).wait_recv()
        to_core(k, 1).wait_recv()

    contract = (((1,), (1,)), ((), ()))

    def rows_of_chunk(k):
        first_slot, slots = CHUNKS[k]
        return pl.ds(first_slot * CAP, slots * CAP)

    def share_to_core(k, j):
        rows = rows_of_chunk(k)
        return remote(
            shares.at[3 - 2 * j, rows], from_core.at[j, rows], rc_send.at[k, j], rc_recv.at[k, j], other_core
        )

    def sum_to_chip(k):
        rows = rows_of_chunk(k)
        return remote(for_x.at[rows], from_x.at[rows], rx_send.at[k], rx_recv.at[k], other_chip)

    def compute(k):
        first_slot, slots = CHUNKS[k]
        rows = rows_of_chunk(k)

        def rows_of(top):
            block = held[:, first_slot : first_slot + slots, top : top + CAP, :]
            return block.reshape(4 * slots * CAP, D)

        rows_in, rows_grad = rows_of(0), rows_of(CAP)
        pre_gate = lax.dot_general(rows_in, weights[0:FF_DEV], contract, preferred_element_type=F32)
        pre_up = lax.dot_general(
            rows_in, weights[FF_DEV : 2 * FF_DEV], contract, preferred_element_type=F32
        )
        hidden = lax.dot_general(
            rows_grad, weights[2 * FF_DEV : 3 * FF_DEV], contract, preferred_element_type=F32
        )
        g = jax.nn.sigmoid(pre_gate)
        gate_coef = (hidden * pre_up * g * (1.0 + pre_gate * (1.0 - g))).astype(BF16)
        up_coef = (hidden * pre_gate * g).astype(BF16)
        for n in range(0, D, QUAD):
            total = jnp.dot(gate_coef, weights[0:FF_DEV, n : n + QUAD], preferred_element_type=F32)
            total = total + jnp.dot(
                up_coef, weights[FF_DEV : 2 * FF_DEV, n : n + QUAD], preferred_element_type=F32
            )
            shares[:, rows, n : n + QUAD] = total.astype(BF16).reshape(4, slots * CAP, QUAD)
        for j in range(2):
            share_to_core(k, j).start()

    def reduce(k):
        rows = rows_of_chunk(k)
        share_to_core(k, 0).wait_recv()
        for_x[rows] = (shares[2, rows].astype(F32) + from_core[0, rows].astype(F32)).astype(BF16)
        sum_to_chip(k).start()

    def finish(k):
        first_slot, slots = CHUNKS[k]
        rows = rows_of_chunk(k)
        share_to_core(k, 1).wait_recv()
        sum_to_chip(k).wait_recv()
        for q in range(4):
            cols = slice(q * QUAD, (q + 1) * QUAD)
            total = (
                shares[0, rows, cols].astype(F32)
                + from_core[1, rows, cols].astype(F32)
                + from_x[rows, cols].astype(F32)
            )
            top = q % 2 * CAP
            returned[q // 2, first_slot : first_slot + slots, top : top + CAP, :] = total.astype(
                BF16
            ).reshape(slots, CAP, QUAD)

    def one_back(side, i):
        src, dst = returned.at[side, i], back.at[side, i]
        if i == 0:
            return pltpu.make_async_copy(src, dst, ret_own.at[side])
        return remote(src, dst, ret_send.at[side, i], ret_recv.at[side, i], peers[i])

    def give_back(side, k):
        first_slot, slots = CHUNKS[k]
        for i in range(first_slot, first_slot + slots):
            one_back(side, i).start()

    for i in NEAR[0::2]:
        arrive(i)
    to_core(0, 0).start()
    send_far()
    for i in NEAR[1::2]:
        arrive(i)
    to_core(1, 0).start()
    gather(0)
    compute(0)
    gather(1)
    compute(1)
    for k in range(2, 6):
        first_slot, slots = CHUNKS[k]
        for i in range(first_slot, first_slot + slots):
            arrive(i)
            if waiting:
                sends[i].wait_send()
                send_far()
        to_core(k, 0).start()
        if k == 2:
            reduce(0)
            reduce(1)
        else:
            reduce(k - 1)
        if k == 5:
            for n in (2, 3):
                give_back(0, n)
        gather(k)
        if k == 5:
            for n in (2, 3):
                give_back(1, n)
        compute(k)
        if k == 3:
            for n in (0, 1):
                finish(n)
                for side in range(2):
                    give_back(side, n)
            finish(2)
        if k == 4:
            finish(3)
    finish(4)
    give_back(0, 4)
    give_back(1, 4)
    reduce(5)
    finish(5)
    give_back(0, 5)
    give_back(1, 5)

    eye = lax.broadcasted_iota(jnp.int32, (tokens, tokens), 0) == lax.broadcasted_iota(
        jnp.int32, (tokens, tokens), 1
    )
    place_col = jnp.sum(jnp.where(eye, place, 0), axis=1, keepdims=True)
    prob_col = jnp.sum(jnp.where(eye, probs_ref[...], 0.0), axis=1, keepdims=True)
    slot = lax.broadcasted_iota(jnp.int32, (tokens, EXPERTS * BLOCK), 1)

    def piece(ref, side, p):
        return ref.at[pl.ds(p % 4 * PIECE, PIECE), pl.ds(side * HALF + p // 4 * QUAD, QUAD)]

    def whole(side):
        cols = pl.ds(side * HALF, HALF)
        return remote(
            result.at[:, cols], out_hbm.at[:, cols], shift_send.at[side], shift_recv.at[side], ahead
        )

    def leg(side, n, j, by):
        p = 2 * n + j
        return remote(
            piece(result, side, p), relay.at[side, j], leg_send.at[side, p], leg_recv.at[side, j],
            ring(PLANES[n], by * NEXT),
        )

    def end(side, n, j, by):
        p = 2 * n + j
        return remote(
            relay.at[side, j], piece(out_hbm, side, p), end_send.at[side, j], end_recv.at[side, p],
            ring(NY - 1, by * (NZ - NEXT)),
        )

    ways = ((0, 1), (1, -1))

    def combine(side):
        for i in range(EXPERTS):
            if i == 0:
                one_back(side, i).wait()
            else:
                one_back(side, i).wait_recv()
        rows_back = back[side].reshape(EXPERTS * BLOCK, QUAD)
        for half in range(2):
            n = side * HALF + half * QUAD
            select = (slot == place_col + half * CAP).astype(BF16)
            own = jnp.dot(select, rows_back, preferred_element_type=F32)
            here = pair[tokens : 2 * tokens, n : n + QUAD].astype(F32)
            result[:, n : n + QUAD] = (here + prob_col * own).astype(BF16)

        @pl.when(jnp.logical_not(first))
        def _():
            whole(side).start()

        @pl.when(first)
        def _():
            for j, by in ways:
                for n in range(len(PLANES)):
                    leg(side, n, j, by).start()

    def pass_on(side, planes):
        for plane in planes:
            n = PLANES.index(plane)

            @pl.when(y == plane)
            def _():
                for j, by in ways:
                    leg(side, n, j, by).wait_recv()
                    end(side, n, j, by).start()

    combine(0)
    pass_on(0, PLANES[1:])
    combine(1)
    pass_on(0, PLANES[:1])
    pass_on(1, PLANES)

    @pl.when(jnp.logical_not(last))
    def _():
        for side in range(2):
            whole(side).wait_recv()

    @pl.when(last)
    def _():
        for side in range(2):
            for j, by in ways:
                for n in range(len(PLANES)):
                    end(side, n, j, by).wait_recv()

    @pl.when(jnp.logical_not(first))
    def _():
        for side in range(2):
            whole(side).wait_send()

    @pl.when(first)
    def _():
        for side in range(2):
            for j, by in ways:
                for n in range(len(PLANES)):
                    leg(side, n, j, by).wait_send()

    @pl.when(relays)
    def _():
        for side in range(2):
            for j, by in ways:
                end(side, 0, j, by).wait_send()

    for k, (first_slot, slots) in enumerate(CHUNKS):
        for j in range(2):
            to_core(k, j).wait_send()
            share_to_core(k, j).wait_send()
        sum_to_chip(k).wait_send()
    for i in range(EXPERTS):
        over_x[i].wait_send()
        if i and not (i in FAR and FAR.index(i) < EXPERTS // 2 - WINDOW):
            sends[i].wait_send()
        for side in range(2):
            if i:
                one_back(side, i).wait_send()


def local(route_ids, route_probs, checkpoints, grad_in, gate_weight, up_weight, down_weight):
    tokens = route_ids.shape[2]
    dma = pltpu.SemaphoreType.DMA
    vmem = pl.BlockSpec(memory_space=pltpu.VMEM)
    hbm = pl.BlockSpec(memory_space=pl.ANY)
    chunks = len(CHUNKS)
    out = pl.pallas_call(
        kernel,
        out_shape=jax.ShapeDtypeStruct((tokens, D), BF16),
        in_specs=[vmem] * 2 + [hbm] * 5,
        out_specs=hbm,
        scratch_shapes=[
            pltpu.VMEM((3 * FF_DEV, D), BF16),
            pltpu.VMEM((2 * tokens, D), BF16),
            pltpu.VMEM((EXPERTS, BLOCK, D), BF16),
            pltpu.VMEM((4, EXPERTS, BLOCK, D), BF16),
            pltpu.VMEM((4, EXPERTS * CAP, D), BF16),
            pltpu.VMEM((2, EXPERTS * CAP, D), BF16),
            pltpu.VMEM((EXPERTS * CAP, D), BF16),
            pltpu.VMEM((EXPERTS * CAP, D), BF16),
            pltpu.VMEM((2, EXPERTS, BLOCK, QUAD), BF16),
            pltpu.VMEM((2, EXPERTS, BLOCK, QUAD), BF16),
            pltpu.VMEM((tokens, D), BF16),
            pltpu.VMEM((2, 2, PIECE, QUAD), BF16),
            dma((3,)), dma((2,)), dma, dma((16,)), dma((16,)), dma((16,)), dma((16,)),
            dma((chunks, 2)), dma((chunks, 2)), dma((chunks, 2)), dma((chunks, 2)),
            dma((chunks,)), dma((chunks,)), dma((2, 16)), dma((2, 16)), dma((2,)),
            dma((2,)), dma((2,)), dma((2, 8)), dma((2, 2)), dma((2, 2)), dma((2, 8)),
        ],
        compiler_params=pltpu.CompilerParams(
            collective_id=0, has_side_effects=True, vmem_limit_bytes=60 * 1024 * 1024
        ),
        cost_estimate=pl.CostEstimate(
            flops=2 * 512 * D * FF_DEV * 5, bytes_accessed=3 * 1024 * 1024, transcendentals=512 * FF_DEV
        ),
    )(
        route_ids.reshape(1, tokens),
        route_probs.reshape(1, tokens),
        checkpoints[0, 0],
        grad_in[0],
        jnp.swapaxes(gate_weight[0], 0, 1),
        jnp.swapaxes(up_weight[0], 0, 1),
        down_weight[0],
    )
    return out[None]


def solution(mesh):
    placed = (
        P(None, "section", "expert", None),
        P(None, "section", "expert", None),
        P(None, "section", "expert", None),
        P("section", "expert", None),
        P("section", None, "expert"),
        P("section", None, "expert"),
        P("section", "expert", None),
    )
    return jax.shard_map(
        local, mesh=mesh, in_specs=placed, out_specs=P("section", "expert", None), check_vma=False
    )
```

```python
import jax
import jax.numpy as jnp
from jax import lax
from jax.experimental import pallas as pl
from jax.experimental.pallas import tpu as pltpu
from jax.sharding import PartitionSpec as P

CAP = 8
BLOCK = 2 * CAP
NZ, NX, NC = 8, 4, 2
EXPERTS = NZ * NX * NC // 4
SECTIONS = 16
FF_DEV = 192
D = 2048
HALF = D // 2
QUAD = D // 4
NY = 8
PIECE = 16
PLANES = (0, NY - 1, 1, NY - 2)
NEXT = 1
NEAR = (0, 8, 1, 9, 2, 10, 3, 11)
FAR = (4, 5, 6, 7, 12, 13, 14, 15)
WINDOW = 5
CHUNKS = ((0, 4), (8, 4), (4, 2), (6, 2), (12, 2), (14, 2))
MESH = pl.DeviceIdType.MESH
F32, BF16 = jnp.float32, jnp.bfloat16


def flipped(z, m):
    out = 0
    for bit in (4, 2, 1):
        b = (z // bit) % 2
        out = out + bit * ((1 - b) if m & bit else b)
    return out


def kernel(
    ids_ref, probs_ref, rows_hbm, grad_hbm, gate_hbm, up_hbm, down_hbm, out_hbm,
    weights, pair, packed, held, shares, from_core, for_x, from_x, returned, back, result, relay,
    load_sem, pair_sem, own_sem, to_sem, at_sem, x_send, x_recv, core_send, core_recv,
    rc_send, rc_recv, rx_send, rx_recv, ret_send, ret_recv, ret_own,
    shift_send, shift_recv, leg_send, leg_recv, end_send, end_recv,
):
    sec = lax.axis_index("section")
    dev = lax.axis_index("expert")
    z, x, c = dev // (NX * NC), (dev // NC) % NX, dev % NC
    y = sec % NY
    depth = (sec // NY) * NZ + z
    tokens = ids_ref.shape[1]

    def at(zz, xx, cc):
        return {"section": sec, "expert": zz * (NX * NC) + xx * NC + cc}

    def ring(yy, by):
        d = (depth + by + 2 * NZ) % (2 * NZ)
        return {
            "section": (d // NZ) * NY + yy,
            "expert": (d % NZ) * (NX * NC) + x * NC + c,
        }

    def remote(src, dst, send, recv, device):
        return pltpu.make_async_remote_copy(
            src_ref=src, dst_ref=dst, send_sem=send, recv_sem=recv,
            device_id=device, device_id_type=MESH,
        )

    other_core = at(z, x, 1 - c)
    other_chip = at(z, x + 1 - 2 * (x % 2), c)
    column = (x, NX - 1 - x)
    peers = [at(flipped(z, i % NZ), column[i // NZ], c) for i in range(EXPERTS)]
    ahead = {"section": (sec + SECTIONS - 1) % SECTIONS, "expert": dev}
    behind = {"section": (sec + 1) % SECTIONS, "expert": dev}
    first, last = y == 0, y == NY - 1
    edge = first | last
    relays = edge | (y == 1) | (y == NY - 2)

    barrier = pltpu.get_barrier_semaphore()

    def greet(device):
        pl.semaphore_signal(barrier, inc=1, device_id=device, device_id_type=MESH)

    partners = peers[1:] + [other_core, other_chip]
    for partner in partners:
        greet(partner)

    @pl.when(y > 0)
    def _():
        greet(ahead)

    @pl.when(y < NY - 1)
    def _():
        greet(behind)

    @pl.when(first)
    def _():
        for plane in PLANES:
            for by in (1, -1):
                greet(ring(plane, by * NEXT))

    @pl.when(relays)
    def _():
        for by in (1, -1):
            greet(ring(0, by * NEXT))
            greet(ring(NY - 1, by * (NZ - NEXT)))

    @pl.when(last)
    def _():
        for plane in PLANES:
            for by in (1, -1):
                greet(ring(plane, by * (NZ - NEXT)))

    takes = [
        pltpu.make_async_copy(src, pair.at[pl.ds(i * tokens, tokens)], pair_sem.at[i])
        for i, src in enumerate((rows_hbm, grad_hbm))
    ]
    loads = [
        pltpu.make_async_copy(src, weights.at[pl.ds(i * FF_DEV, FF_DEV)], load_sem.at[i])
        for i, src in enumerate((gate_hbm, up_hbm, down_hbm))
    ]
    for load in takes + loads:
        load.start()

    ids = ids_ref[...]
    named = (lax.broadcasted_iota(jnp.int32, (EXPERTS, tokens), 0) == ids).astype(F32)
    before = (
        lax.broadcasted_iota(jnp.int32, (tokens, tokens), 0)
        < lax.broadcasted_iota(jnp.int32, (tokens, tokens), 1)
    ).astype(F32)
    earlier = jnp.dot(named, before, preferred_element_type=F32)
    rank = jnp.sum(earlier * named, axis=0, keepdims=True).astype(jnp.int32)
    message = jnp.where(ids % 2 == x // 2, 0, NZ) + jnp.bitwise_xor(ids // 2, z)
    place = message * BLOCK + rank
    row = lax.broadcasted_iota(jnp.int32, (EXPERTS * BLOCK, tokens), 0)
    pick = jnp.concatenate(
        [(row == place).astype(F32), (row == place + CAP).astype(F32)], axis=1
    ).astype(BF16)
    for take in takes:
        take.wait()
    for n in range(0, D, QUAD):
        packed[:, :, n : n + QUAD] = (
            jnp.dot(pick, pair[:, n : n + QUAD], preferred_element_type=F32)
            .astype(BF16)
            .reshape(EXPERTS, BLOCK, QUAD)
        )

    pairs = 2 * len(PLANES)

    @pl.when(edge)
    def _():
        pl.semaphore_wait(barrier, len(partners) + pairs + 5)

    @pl.when(relays & jnp.logical_not(edge))
    def _():
        pl.semaphore_wait(barrier, len(partners) + 6)

    @pl.when(jnp.logical_not(relays))
    def _():
        pl.semaphore_wait(barrier, len(partners) + 2)

    sends = [pltpu.make_async_copy(packed.at[0], held.at[0, 0], own_sem)] + [
        remote(packed.at[i], held.at[0, i], to_sem.at[i], at_sem.at[i], peers[i])
        for i in range(1, EXPERTS)
    ]
    over_x = [
        remote(held.at[0, i], held.at[2, i], x_send.at[i], x_recv.at[i], other_chip)
        for i in range(EXPERTS)
    ]
    waiting = list(FAR)

    def send_far():
        if waiting:
            sends[waiting.pop(0)].start()

    for _ in range(WINDOW - 1):
        send_far()
    for i in NEAR:
        sends[i].start()

    for load in loads:
        load.wait()

    def arrive(i):
        if i == 0:
            sends[i].wait()
        else:
            sends[i].wait_recv()
        over_x[i].start()

    def to_core(k, j):
        first_slot, slots = CHUNKS[k]
        many = pl.ds(first_slot, slots)
        return remote(
            held.at[2 * j, many], held.at[2 * j + 1, many], core_send.at[k, j], core_recv.at[k, j], other_core
        )

    def gather(k):
        first_slot, slots = CHUNKS[k]
        for i in range(first_slot, first_slot + slots):
            over_x[i].wait_recv()
        to_core(k, 1).start()
        to_core(k, 0).wait_recv()
        to_core(k, 1).wait_recv()

    contract = (((1,), (1,)), ((), ()))

    def rows_of_chunk(k):
        first_slot, slots = CHUNKS[k]
        return pl.ds(first_slot * CAP, slots * CAP)

    def share_to_core(k, j):
        rows = rows_of_chunk(k)
        return remote(
            shares.at[3 - 2 * j, rows], from_core.at[j, rows], rc_send.at[k, j], rc_recv.at[k, j], other_core
        )

    def sum_to_chip(k):
        rows = rows_of_chunk(k)
        return remote(for_x.at[rows], from_x.at[rows], rx_send.at[k], rx_recv.at[k], other_chip)

    def compute(k):
        first_slot, slots = CHUNKS[k]
        rows = rows_of_chunk(k)

        def rows_of(top):
            block = held[:, first_slot : first_slot + slots, top : top + CAP, :]
            return block.reshape(4 * slots * CAP, D)

        rows_in, rows_grad = rows_of(0), rows_of(CAP)
        pre_gate = lax.dot_general(rows_in, weights[0:FF_DEV], contract, preferred_element_type=F32)
        pre_up = lax.dot_general(
            rows_in, weights[FF_DEV : 2 * FF_DEV], contract, preferred_element_type=F32
        )
        hidden = lax.dot_general(
            rows_grad, weights[2 * FF_DEV : 3 * FF_DEV], contract, preferred_element_type=F32
        )
        g = jax.nn.sigmoid(pre_gate)
        gate_coef = (hidden * pre_up * g * (1.0 + pre_gate * (1.0 - g))).astype(BF16)
        up_coef = (hidden * pre_gate * g).astype(BF16)
        for n in range(0, D, QUAD):
            total = jnp.dot(gate_coef, weights[0:FF_DEV, n : n + QUAD], preferred_element_type=F32)
            total = total + jnp.dot(
                up_coef, weights[FF_DEV : 2 * FF_DEV, n : n + QUAD], preferred_element_type=F32
            )
            shares[:, rows, n : n + QUAD] = total.astype(BF16).reshape(4, slots * CAP, QUAD)
        for j in range(2):
            share_to_core(k, j).start()

    def reduce(k):
        rows = rows_of_chunk(k)
        share_to_core(k, 0).wait_recv()
        for_x[rows] = (shares[2, rows].astype(F32) + from_core[0, rows].astype(F32)).astype(BF16)
        sum_to_chip(k).start()

    def finish(k):
        first_slot, slots = CHUNKS[k]
        rows = rows_of_chunk(k)
        share_to_core(k, 1).wait_recv()
        sum_to_chip(k).wait_recv()
        for q in range(4):
            cols = slice(q * QUAD, (q + 1) * QUAD)
            total = (
                shares[0, rows, cols].astype(F32)
                + from_core[1, rows, cols].astype(F32)
                + from_x[rows, cols].astype(F32)
            )
            top = q % 2 * CAP
            returned[q // 2, first_slot : first_slot + slots, top : top + CAP, :] = total.astype(
                BF16
            ).reshape(slots, CAP, QUAD)

    def one_back(side, i):
        src, dst = returned.at[side, i], back.at[side, i]
        if i == 0:
            return pltpu.make_async_copy(src, dst, ret_own.at[side])
        return remote(src, dst, ret_send.at[side, i], ret_recv.at[side, i], peers[i])

    def give_back(side, k):
        first_slot, slots = CHUNKS[k]
        for i in range(first_slot, first_slot + slots):
            one_back(side, i).start()

    for i in NEAR[0::2]:
        arrive(i)
    to_core(0, 0).start()
    send_far()
    for i in NEAR[1::2]:
        arrive(i)
    to_core(1, 0).start()
    gather(0)
    compute(0)
    gather(1)
    compute(1)
    def far(k):
        first_slot, slots = CHUNKS[k]
        for i in range(first_slot, first_slot + slots):
            arrive(i)
            if waiting:
                sends[i].wait_send()
                send_far()
        to_core(k, 0).start()

    far(2)
    reduce(0)
    reduce(1)
    far(3)
    gather(2)
    compute(2)
    for n in (0, 1):
        finish(n)
        for side in range(2):
            give_back(side, n)
    far(4)
    reduce(2)
    gather(3)
    compute(3)
    finish(2)
    far(5)
    give_back(0, 2)
    reduce(3)
    gather(4)
    compute(4)
    finish(3)
    give_back(0, 3)
    gather(5)
    compute(5)
    give_back(1, 2)
    reduce(4)
    give_back(1, 3)
    reduce(5)
    finish(4)
    for side in range(2):
        give_back(side, 4)
    finish(5)
    for side in range(2):
        give_back(side, 5)

    eye = lax.broadcasted_iota(jnp.int32, (tokens, tokens), 0) == lax.broadcasted_iota(
        jnp.int32, (tokens, tokens), 1
    )
    place_col = jnp.sum(jnp.where(eye, place, 0), axis=1, keepdims=True)
    prob_col = jnp.sum(jnp.where(eye, probs_ref[...], 0.0), axis=1, keepdims=True)
    slot = lax.broadcasted_iota(jnp.int32, (tokens, EXPERTS * BLOCK), 1)

    def piece(ref, side, p):
        return ref.at[pl.ds(p % 4 * PIECE, PIECE), pl.ds(side * HALF + p // 4 * QUAD, QUAD)]

    def whole(side):
        cols = pl.ds(side * HALF, HALF)
        return remote(
            result.at[:, cols], out_hbm.at[:, cols], shift_send.at[side], shift_recv.at[side], ahead
        )

    def leg(side, n, j, by):
        p = 2 * n + j
        return remote(
            piece(result, side, p), relay.at[side, j], leg_send.at[side, p], leg_recv.at[side, j],
            ring(PLANES[n], by * NEXT),
        )

    def end(side, n, j, by):
        p = 2 * n + j
        return remote(
            relay.at[side, j], piece(out_hbm, side, p), end_send.at[side, j], end_recv.at[side, p],
            ring(NY - 1, by * (NZ - NEXT)),
        )

    ways = ((0, 1), (1, -1))

    def combine(side):
        for i in range(EXPERTS):
            if i == 0:
                one_back(side, i).wait()
            else:
                one_back(side, i).wait_recv()
        rows_back = back[side].reshape(EXPERTS * BLOCK, QUAD)
        for half in range(2):
            n = side * HALF + half * QUAD
            select = (slot == place_col + half * CAP).astype(BF16)
            own = jnp.dot(select, rows_back, preferred_element_type=F32)
            here = pair[tokens : 2 * tokens, n : n + QUAD].astype(F32)
            result[:, n : n + QUAD] = (here + prob_col * own).astype(BF16)

        @pl.when(jnp.logical_not(first))
        def _():
            whole(side).start()

        @pl.when(first)
        def _():
            for j, by in ways:
                for n in range(len(PLANES)):
                    leg(side, n, j, by).start()

    def pass_on(side, planes):
        for plane in planes:
            n = PLANES.index(plane)

            @pl.when(y == plane)
            def _():
                for j, by in ways:
                    leg(side, n, j, by).wait_recv()
                    end(side, n, j, by).start()

    combine(0)
    pass_on(0, PLANES[1:])
    combine(1)
    pass_on(0, PLANES[:1])
    pass_on(1, PLANES)

    @pl.when(jnp.logical_not(last))
    def _():
        for side in range(2):
            whole(side).wait_recv()

    @pl.when(last)
    def _():
        for side in range(2):
            for j, by in ways:
                for n in range(len(PLANES)):
                    end(side, n, j, by).wait_recv()

    @pl.when(jnp.logical_not(first))
    def _():
        for side in range(2):
            whole(side).wait_send()

    @pl.when(first)
    def _():
        for side in range(2):
            for j, by in ways:
                for n in range(len(PLANES)):
                    leg(side, n, j, by).wait_send()

    @pl.when(relays)
    def _():
        for side in range(2):
            for j, by in ways:
                end(side, 0, j, by).wait_send()

    for k, (first_slot, slots) in enumerate(CHUNKS):
        for j in range(2):
            to_core(k, j).wait_send()
            share_to_core(k, j).wait_send()
        sum_to_chip(k).wait_send()
    for i in range(EXPERTS):
        over_x[i].wait_send()
        if i and not (i in FAR and FAR.index(i) < EXPERTS // 2 - WINDOW):
            sends[i].wait_send()
        for side in range(2):
            if i:
                one_back(side, i).wait_send()


def local(route_ids, route_probs, checkpoints, grad_in, gate_weight, up_weight, down_weight):
    tokens = route_ids.shape[2]
    dma = pltpu.SemaphoreType.DMA
    vmem = pl.BlockSpec(memory_space=pltpu.VMEM)
    hbm = pl.BlockSpec(memory_space=pl.ANY)
    chunks = len(CHUNKS)
    out = pl.pallas_call(
        kernel,
        out_shape=jax.ShapeDtypeStruct((tokens, D), BF16),
        in_specs=[vmem] * 2 + [hbm] * 5,
        out_specs=hbm,
        scratch_shapes=[
            pltpu.VMEM((3 * FF_DEV, D), BF16),
            pltpu.VMEM((2 * tokens, D), BF16),
            pltpu.VMEM((EXPERTS, BLOCK, D), BF16),
            pltpu.VMEM((4, EXPERTS, BLOCK, D), BF16),
            pltpu.VMEM((4, EXPERTS * CAP, D), BF16),
            pltpu.VMEM((2, EXPERTS * CAP, D), BF16),
            pltpu.VMEM((EXPERTS * CAP, D), BF16),
            pltpu.VMEM((EXPERTS * CAP, D), BF16),
            pltpu.VMEM((2, EXPERTS, BLOCK, QUAD), BF16),
            pltpu.VMEM((2, EXPERTS, BLOCK, QUAD), BF16),
            pltpu.VMEM((tokens, D), BF16),
            pltpu.VMEM((2, 2, PIECE, QUAD), BF16),
            dma((3,)), dma((2,)), dma, dma((16,)), dma((16,)), dma((16,)), dma((16,)),
            dma((chunks, 2)), dma((chunks, 2)), dma((chunks, 2)), dma((chunks, 2)),
            dma((chunks,)), dma((chunks,)), dma((2, 16)), dma((2, 16)), dma((2,)),
            dma((2,)), dma((2,)), dma((2, 8)), dma((2, 2)), dma((2, 2)), dma((2, 8)),
        ],
        compiler_params=pltpu.CompilerParams(
            collective_id=0, has_side_effects=True, vmem_limit_bytes=60 * 1024 * 1024
        ),
        cost_estimate=pl.CostEstimate(
            flops=2 * 512 * D * FF_DEV * 5, bytes_accessed=3 * 1024 * 1024, transcendentals=512 * FF_DEV
        ),
    )(
        route_ids.reshape(1, tokens),
        route_probs.reshape(1, tokens),
        checkpoints[0, 0],
        grad_in[0],
        jnp.swapaxes(gate_weight[0], 0, 1),
        jnp.swapaxes(up_weight[0], 0, 1),
        down_weight[0],
    )
    return out[None]


def solution(mesh):
    placed = (
        P(None, "section", "expert", None),
        P(None, "section", "expert", None),
        P(None, "section", "expert", None),
        P("section", "expert", None),
        P("section", None, "expert"),
        P("section", None, "expert"),
        P("section", "expert", None),
    )
    return jax.shard_map(
        local, mesh=mesh, in_specs=placed, out_specs=P("section", "expert", None), check_vma=False
    )
```
